32 devices in a mesh: src: 4 (over z), dst: 4 (over y, core), rel: 2 (over x).
Axes of the slice: x: 2, y: 2, z: 4, core: 2. Of those that a mesh axis runs over, the one named last changes fastest.
Arguments:
- features: bfloat16 [2048, 512], P(('src', 'dst')), may hold values from -6 to 6
- out_grad: bfloat16 [2048, 512], P(('dst', 'src')), may hold values from -6 to 6
- weights: bfloat16 [2, 512, 512], P('rel'), may hold values from -0.25 to 0.25
- tiles: bfloat16 [2, 64, 128, 128], P('rel', ('src', 'dst')), may hold values from 0 to 1.5, as said below
- tile_rows: int32 [2, 64], P('rel', ('src', 'dst')), may hold values from 0 to 3
- tile_cols: int32 [2, 64], P('rel', ('src', 'dst')), may hold values from 0 to 3
- tile_count: int32 [2, 16], P('rel', ('src', 'dst')), may hold values from 1 to 4, as said below
- degrees: int32 [2, 2048], P('rel', ('dst', 'src')), may hold values from 1 to 64
Outputs:
- feature_grad: bfloat16 [2048, 512], P(('src', 'dst'))
- weight_grad: float32 [2, 512, 512], P('rel')
The draws below stay inside these ranges and needn't reach their ends.
Inputs may be any that keep to these rules, and one draw needn't show every extreme that they name: An edge weight where an edge exists, else 0; the live tiles of one pair of panels lie at distinct positions. `tile_count`: the live slots are the first ones; pair 0 of every relation is full.
All inputs are finite; a program needn't handle non-finite values.
Results may differ from the reference program's by a relative error of at most 0.0024.
Values may be sent and summed in bfloat16 or wider, within the bound.
A program may use at most 64 MiB of HBM per device.

```python
import jax
import jax.numpy as jnp
from jax import lax

D = 512
TILE = 128
ROWS_DEV = 128
RELS = 2
DEV_BLOCKS = 16
NODES = 2048
TILE_ROWS = 4
TILE_COLS = 4
TILES_DEV = 4
N_SRC = 4
N_DST = 4


def tile_positions(key):
    keys = jax.random.split(key, RELS * DEV_BLOCKS)
    order = jax.vmap(lambda single: jax.random.permutation(single, TILE_ROWS * TILE_COLS))(keys)
    return order[:, :TILES_DEV].reshape(RELS, DEV_BLOCKS * TILES_DEV).astype(jnp.int32)


def draw_tile_rows(key, part):
    order = tile_positions(key)
    return order // TILE_COLS


def draw_tile_cols(key, part):
    order = tile_positions(key)
    return order % TILE_COLS


def draw_tiles(key, part):
    key = jax.random.fold_in(key, 3)
    shape = (RELS, DEV_BLOCKS * TILES_DEV, TILE, TILE)
    edge_key, value_key = jax.random.split(key)
    present = jax.random.bernoulli(edge_key, 1.0 / 3.0, shape).astype(jnp.float32)
    values = jax.random.uniform(value_key, shape, jnp.float32, 0.5, 1.5)
    return (present * values).astype(jnp.bfloat16)


def draw_tile_count(key, part):
    key = jax.random.fold_in(key, 5)
    shifts = jax.random.randint(key, (RELS, DEV_BLOCKS), 0, 3)
    counts = jnp.right_shift(jnp.full((RELS, DEV_BLOCKS), TILES_DEV, jnp.int32), shifts)
    return counts.at[:, 0].set(TILES_DEV).astype(jnp.int32)


def draw_degrees(key, part):
    key = jax.random.fold_in(key, 7)
    base_key, shift_key = jax.random.split(key)
    base = jax.random.randint(base_key, (RELS, NODES), 1, 5)
    shifts = jax.random.randint(shift_key, (RELS, NODES), 0, 5)
    return jnp.left_shift(base, shifts).astype(jnp.int32)


def level_of(own_key, shape, cuts, smallest, largest):
    loudness = 1.0
    for axis_at, parts in cuts:
        draws = jax.random.uniform(jax.random.fold_in(jax.random.fold_in(own_key, 6), axis_at), (parts,), jnp.float32, smallest / len(cuts), largest / len(cuts))
        loudness = loudness * jnp.repeat(jnp.exp(draws), shape[axis_at] // parts).reshape((-1,) + (1,) * (len(shape) - 1 - axis_at))
    return loudness


def noise(key, dims, spread, reach, cuts=(), kind=jnp.bfloat16):
    values = jax.random.normal(key, dims, jnp.float32) * spread
    if len(cuts) > 0:
        values = level_of(key, dims, cuts, -0.22, 0.18) * values
    return jnp.clip(values, min=-reach, max=reach).astype(kind)


def setup_inputs(seed: int = 0) -> dict:
    splits = jax.random.split(jax.random.key(seed), 9)
    return {
        "features": noise(splits[0], (NODES, D), 1.0, 6.0, ((0, 16),)),
        "out_grad": noise(splits[1], (NODES, D), 1.0, 6.0, ((0, 16),)),
        "weights": noise(splits[2], (RELS, D, D), D ** -0.5, 0.25, ((0, 2),)),
        "tiles": draw_tiles(jax.random.fold_in(splits[8], 71), 0),
        "tile_rows": draw_tile_rows(jax.random.fold_in(splits[8], 71), 0),
        "tile_cols": draw_tile_cols(jax.random.fold_in(splits[8], 71), 0),
        "tile_count": draw_tile_count(jax.random.fold_in(splits[8], 71), 0),
        "degrees": draw_degrees(jax.random.fold_in(splits[8], 71), 0),
    }


def reference(features, out_grad, weights, tiles, tile_rows, tile_cols, tile_count, degrees):
    dst_width = ROWS_DEV * N_SRC
    src_width = ROWS_DEV * N_DST
    feature_sum = jnp.zeros((NODES, D), jnp.float32)
    weight_list = []
    features_wide = features.astype(jnp.float32)
    for relation in range(RELS):
        scaled = (out_grad.astype(jnp.float32) / degrees[relation].astype(jnp.float32)[:, None]).astype(jnp.bfloat16)

        def one_source(src_index):
            def one_dest(total, dst_index):
                block = src_index * N_DST + dst_index
                start = (block * TILES_DEV).astype(jnp.int32)
                tile_set = lax.dynamic_slice_in_dim(tiles[relation], start, TILES_DEV, 0)
                row_set = lax.dynamic_slice_in_dim(tile_rows[relation], start, TILES_DEV, 0)
                col_set = lax.dynamic_slice_in_dim(tile_cols[relation], start, TILES_DEV, 0)
                panel = lax.dynamic_slice_in_dim(scaled, (dst_index * dst_width).astype(jnp.int32), dst_width, 0)
                picked = panel.reshape(TILE_ROWS, TILE, D)[row_set]
                contrib = jnp.einsum("gij,gjd->gid", tile_set.astype(jnp.float32), picked.astype(jnp.float32))
                valid = jnp.arange(TILES_DEV, dtype=jnp.int32) < tile_count[relation, block]
                select = ((col_set[:, None] == jnp.arange(TILE_COLS, dtype=jnp.int32)[None, :]) & valid[:, None]).astype(jnp.float32)
                added = jnp.einsum("gc,gid->cid", select, contrib, precision=lax.Precision.HIGHEST)
                return total + added, None

            empty = jnp.zeros((TILE_COLS, TILE, D), jnp.float32)
            total, unused = lax.scan(one_dest, empty, jnp.arange(N_DST, dtype=jnp.int32))
            return total.reshape(src_width, D)

        reduced = lax.map(one_source, jnp.arange(N_SRC, dtype=jnp.int32)).reshape(NODES, D)
        weight_wide = weights[relation].astype(jnp.float32)
        feature_sum = feature_sum + jnp.dot(reduced, weight_wide.T, precision=lax.Precision.HIGHEST)
        weight_list.append(jnp.dot(features_wide.T, reduced, precision=lax.Precision.HIGHEST))
    return feature_sum.astype(jnp.bfloat16), jnp.stack(weight_list)
```

```python
import jax
import jax.numpy as jnp
from jax import lax
from jax.experimental import pallas as pl
from jax.experimental.pallas import tpu as pltpu
from jax.sharding import PartitionSpec as P

MESH = pl.DeviceIdType.MESH
B = 128
F32, BF16 = jnp.float32, jnp.bfloat16


def split_high_low(x):
    high = x.astype(BF16)
    return high, (x - high.astype(F32)).astype(BF16)


def kernel(
    feat_ref, grad_ref, weight_ref, tiles_ref, rows_ref, cols_ref, count_ref, deg_ref,
    fgrad_ref, wgrad_ref,
    own, scal, meta, feats, feats_t, dense, red, rows_f32, wpart, wrecv, final, mine, other,
    a_send, a_recv, t_send, t_recv, f_send, f_recv, c_send, c_recv, d_send, d_recv,
    z_send, z_recv, y_send, y_recv, k_send, k_recv, g_send, g_recv, r_send, r_recv, x_send, x_recv,
):
    s, d, r = lax.axis_index("src"), lax.axis_index("dst"), lax.axis_index("rel")
    peer = (d, d + 1 - 2 * (d % 2), (d + 2) % 4, 3 - d)

    def zpos(step):
        return (s + step) % 4

    def to(source, target, send, recv, **device):
        return pltpu.make_async_remote_copy(
            src_ref=source, dst_ref=target, send_sem=send, recv_sem=recv,
            device_id=device, device_id_type=MESH,
        )

    barrier = pltpu.get_barrier_semaphore()
    for j in (1, 2, 3):
        pl.semaphore_signal(barrier, inc=1, device_id={"dst": peer[j]}, device_id_type=MESH)
        pl.semaphore_signal(barrier, inc=1, device_id={"src": zpos(j)}, device_id_type=MESH)
    pl.semaphore_signal(barrier, inc=1, device_id={"rel": 1 - r}, device_id_type=MESH)

    deg = jnp.broadcast_to(deg_ref[...].astype(F32), (B, B)).T
    for slab in range(4):
        own[slab] = (grad_ref[:, slab * B : (slab + 1) * B].astype(F32) / deg).astype(BF16)
    line = lax.broadcasted_iota(jnp.int32, (16, B), 0)
    place = jnp.full((16, B), -1, jnp.int32)
    for t in range(4):
        meta[0, t * B : (t + 1) * B, :] = tiles_ref[t]
        where_t = rows_ref[0, t] * 4 + cols_ref[0, t]
        place = jnp.where((line == t) & (t < count_ref[0, 0]), where_t, place)
    meta[0, 4 * B : 4 * B + 16, :] = place.astype(F32).astype(BF16)
    feats[0] = feat_ref[...]
    scal[s, 0] = own[d]

    pl.semaphore_wait(barrier, 7)

    sent = []

    def go(copy):
        copy.start()
        sent.append(copy)
        return copy

    slabs = [
        go(to(own.at[peer[j]], scal.at[s, j], a_send.at[j], a_recv.at[j], dst=peer[j]))
        for j in (1, 2, 3)
    ]
    tile_y = go(to(meta.at[0], meta.at[2], t_send.at[2], t_recv.at[2], dst=peer[2]))
    tile_k = go(to(meta.at[0], meta.at[1], t_send.at[1], t_recv.at[1], dst=peer[1]))
    feat_y = go(to(feats.at[0], feats.at[2], f_send.at[2], f_recv.at[2], dst=peer[2]))
    feat_k = go(to(feats.at[0], feats.at[1], f_send.at[1], f_recv.at[1], dst=peer[1]))
    for copy in slabs:
        copy.wait_recv()
    gathers = [
        go(to(scal.at[s], scal.at[s], c_send.at[j], c_recv.at[j], src=zpos(j)))
        for j in (1, 2, 3)
    ]

    def densify(j):
        for k in range(4):
            for c in range(4):
                total = None
                for t in range(4):
                    code = meta[j, 4 * B + t : 4 * B + t + 1, :].astype(F32)
                    hit = jnp.where(code == (k * 4 + peer[c]).astype(F32), 1.0, 0.0).astype(BF16)
                    term = meta[j, t * B : (t + 1) * B, :] * hit
                    total = term if total is None else total + term
                dense[k, c * B : (c + 1) * B, j * B : (j + 1) * B] = total

    densify(0)
    tile_k.wait_recv()
    densify(1)
    tile_y.wait_recv()
    tile_g = go(to(meta.at[2], meta.at[3], t_send.at[3], t_recv.at[3], dst=peer[1]))
    densify(2)
    feat_y.wait_recv()
    feat_g = go(to(feats.at[2], feats.at[3], f_send.at[3], f_recv.at[3], dst=peer[1]))
    feat_k.wait_recv()
    tile_g.wait_recv()
    densify(3)
    for j in range(3):
        feats_t[:, j * B : (j + 1) * B] = feats[j].T
    feat_g.wait_recv()
    feats_t[:, 3 * B :] = feats[3].T

    def block_sum(at):
        return jnp.dot(dense[at], scal[at].reshape(4 * B, B), preferred_element_type=F32)

    total = block_sum(s)
    for j in (1, 3, 2):
        gathers[j - 1].wait_recv()
        total = total + block_sum(zpos(4 - j))
    for c in range(4):
        red[c] = total[c * B : (c + 1) * B]
    rows_f32[d] = red[0]
    rows = [
        go(to(red.at[j], rows_f32.at[d], r_send.at[j], r_recv.at[j], dst=peer[j]))
        for j in (1, 2, 3)
    ]
    high, low = split_high_low(total)
    for c in range(4):
        left = feats_t[c * B : (c + 1) * B, :]
        wpart[c] = jnp.dot(left, high, preferred_element_type=F32) + jnp.dot(
            left, low, preferred_element_type=F32
        )
    parts = [
        go(to(wpart.at[zpos(j)], wrecv.at[j], d_send.at[j], d_recv.at[j], src=zpos(j)))
        for j in (1, 2, 3)
    ]
    for copy in rows:
        copy.wait_recv()
    value = None
    for c in range(4):
        right = weight_ref[:, c * B : (c + 1) * B]
        for part in split_high_low(rows_f32[c]):
            term = lax.dot_general(part, right, (((1,), (1,)), ((), ())), preferred_element_type=F32)
            value = term if value is None else value + term
    mine[...] = value
    swap = go(to(mine, other, x_send.at[0], x_recv.at[0], rel=1 - r))
    block = wpart[s]
    for copy in parts:
        copy.wait_recv()
    block = block + wrecv[1] + wrecv[2] + wrecv[3]
    final[d, s] = block.astype(BF16)

    along = [
        go(to(final.at[d, s], final.at[d, s], z_send.at[j], z_recv.at[j], src=zpos(j)))
        for j in (1, 2, 3)
    ]
    ys, ks, gs = [], [], []
    order = (0, 1, 3, 2)
    for j in order:
        if j:
            along[j - 1].wait_recv()
        at = final.at[d, zpos(4 - j)]
        ys.append(go(to(at, at, y_send.at[j], y_recv.at[j], dst=peer[2])))
        ks.append(go(to(at, at, k_send.at[j], k_recv.at[j], dst=peer[1])))
    for n, j in enumerate(order):
        ys[n].wait_recv()
        at = final.at[peer[2], zpos(4 - j)]
        gs.append(go(to(at, at, g_send.at[j], g_recv.at[j], dst=peer[1])))
    swap.wait_recv()
    fgrad_ref[...] = (mine[...] + other[...]).astype(BF16)
    for copy in ks + gs:
        copy.wait_recv()
    for slab in range(4):
        for q in range(4):
            wgrad_ref[q * B : (q + 1) * B, slab * B : (slab + 1) * B] = final[slab, q]
    for copy in sent:
        copy.wait_send()


def fast_body(features, out_grad, weights, tiles, tile_rows, tile_cols, tile_count, degrees):
    vmem = pl.BlockSpec(memory_space=pltpu.VMEM)
    smem = pl.BlockSpec(memory_space=pltpu.SMEM)
    sem = pltpu.SemaphoreType.DMA((4,))
    fgrad, wgrad = pl.pallas_call(
        kernel,
        out_shape=(
            jax.ShapeDtypeStruct((B, 4 * B), BF16),
            jax.ShapeDtypeStruct((4 * B, 4 * B), BF16),
        ),
        in_specs=[vmem, vmem, vmem, vmem, smem, smem, smem, vmem],
        out_specs=(vmem, vmem),
        scratch_shapes=[
            pltpu.VMEM((4, B, B), BF16),
            pltpu.VMEM((4, 4, B, B), BF16),
            pltpu.VMEM((4, 4 * B + 16, B), BF16),
            pltpu.VMEM((4, B, 4 * B), BF16),
            pltpu.VMEM((4 * B, 4 * B), BF16),
            pltpu.VMEM((4, 4 * B, 4 * B), BF16),
            pltpu.VMEM((4, B, B), F32),
            pltpu.VMEM((4, B, B), F32),
            pltpu.VMEM((4, B, B), F32),
            pltpu.VMEM((4, B, B), F32),
            pltpu.VMEM((4, 4, B, B), BF16),
            pltpu.VMEM((B, 4 * B), F32),
            pltpu.VMEM((B, 4 * B), F32),
        ]
        + [sem] * 22,
        compiler_params=pltpu.CompilerParams(
            collective_id=0, has_side_effects=True, vmem_limit_bytes=32 * 1024 * 1024
        ),
        cost_estimate=pl.CostEstimate(flops=10**9, bytes_accessed=4 * 10**6, transcendentals=0),
    )(features, out_grad, weights[0], tiles[0], tile_rows, tile_cols, tile_count, degrees)
    return fgrad, wgrad.astype(F32)[None]


def body(features, out_grad, weights, tiles, tile_rows, tile_cols, tile_count, degrees):
    tile_size = tiles.shape[-1]
    width = features.shape[1]
    rows_dev = features.shape[0]
    n_dst = lax.axis_size("dst")
    n_cols = rows_dev * n_dst // tile_size
    group_size = 4
    scaled = (out_grad.astype(jnp.float32) / degrees[0].astype(jnp.float32)[:, None]).astype(
        jnp.bfloat16
    )
    panel = lax.all_gather(scaled, "src", axis=0, tiled=True)
    blocks = panel.reshape(-1, tile_size, width)
    live_count = tile_count[0, 0]

    def add_group(index, total):
        start = index * group_size
        tile_group = lax.dynamic_slice_in_dim(tiles[0], start, group_size, 0)
        row_group = lax.dynamic_slice_in_dim(tile_rows[0], start, group_size, 0)
        col_group = lax.dynamic_slice_in_dim(tile_cols[0], start, group_size, 0)
        picked = jnp.take(blocks, row_group, axis=0)
        contrib = jnp.einsum("gij,gjd->gid", tile_group, picked, preferred_element_type=jnp.float32)
        valid = (start + jnp.arange(group_size, dtype=jnp.int32) < live_count).astype(jnp.float32)
        return total.at[col_group].add(contrib * valid[:, None, None])

    n_groups = (live_count + group_size - 1) // group_size
    empty = jnp.zeros((n_cols, tile_size, width), jnp.float32)
    summed = lax.fori_loop(0, n_groups, add_group, empty)
    partial_value = summed.reshape(n_cols * tile_size, width)
    reduced = lax.psum_scatter(partial_value, "dst", scatter_dimension=0, tiled=True)
    local_weight = jnp.dot(features.astype(jnp.float32).T, reduced, precision=lax.Precision.HIGHEST)
    weight_grad = lax.psum(local_weight, ("src", "dst"))
    weight_wide = weights[0].astype(jnp.float32)
    own_part = jnp.dot(reduced, weight_wide.T, precision=lax.Precision.HIGHEST)
    feature_grad = lax.psum(own_part, "rel").astype(jnp.bfloat16)
    return (feature_grad, weight_grad[None])


def solution(mesh):
    in_specs = (
        P(("src", "dst"), None),
        P(("dst", "src"), None),
        P("rel", None, None),
        P("rel", ("src", "dst"), None, None),
        P("rel", ("src", "dst")),
        P("rel", ("src", "dst")),
        P("rel", ("src", "dst")),
        P("rel", ("dst", "src")),
    )
    out_specs = (P(("src", "dst"), None), P("rel", None, None))
    sizes = (mesh.shape["src"], mesh.shape["dst"], mesh.shape["rel"])

    def run(*args):
        features, tiles = args[0], args[3]
        shapes = (features.shape, tiles.shape)
        small = sizes == (4, 4, 2) and shapes == ((16 * B, 4 * B), (2, 64, B, B))
        chosen = fast_body if small else body
        return jax.shard_map(
            chosen, mesh=mesh, in_specs=in_specs, out_specs=out_specs, check_vma=False
        )(*args)

    return run
```

```python
import jax
import jax.numpy as jnp
from jax import lax
from jax.experimental import pallas as pl
from jax.experimental.pallas import tpu as pltpu
from jax.sharding import PartitionSpec as P

MESH = pl.DeviceIdType.MESH
B = 128
F32, BF16 = jnp.float32, jnp.bfloat16


def split_high_low(x):
    high = x.astype(BF16)
    return high, (x - high.astype(F32)).astype(BF16)


def kernel(
    feat_ref, grad_ref, weight_ref, tiles_ref, rows_ref, cols_ref, count_ref, deg_ref,
    fgrad_ref, wgrad_ref,
    grad, weight, deg_in, rows_in, cols_in, count_in, total, own, scal, meta, feats, feats_t, dense, red, rows_f32, wpart, wrecv, final, mine, other,
    l_sem, right_send, left_send, c_recv, a_send, a_recv, t_send, t_recv, f_send, f_recv, d_send, d_recv,
    z_send, z_recv, y_send, y_recv, k_send, k_recv, g_send, g_recv, r_send, r_recv, x_send, x_recv,
):
    s, d, r = lax.axis_index("src"), lax.axis_index("dst"), lax.axis_index("rel")
    peer = (d, d + 1 - 2 * (d % 2), (d + 2) % 4, 3 - d)

    def zpos(step):
        return (s + step) % 4

    def to(source, target, send, recv, **device):
        return pltpu.make_async_remote_copy(
            src_ref=source, dst_ref=target, send_sem=send, recv_sem=recv,
            device_id=device, device_id_type=MESH,
        )

    loads = [
        pltpu.make_async_copy(source, target, l_sem.at[n])
        for n, (source, target) in enumerate((
            (grad_ref, grad), (deg_ref, deg_in), (rows_ref, rows_in), (cols_ref, cols_in),
            (count_ref, count_in), (tiles_ref, meta.at[0, pl.ds(0, 4 * B)]),
            (feat_ref, feats.at[0]), (weight_ref, weight),
        ))
    ]
    for copy in loads:
        copy.start()
    barrier = pltpu.get_barrier_semaphore()
    for j in (1, 2, 3):
        pl.semaphore_signal(barrier, inc=1, device_id={"dst": peer[j]}, device_id_type=MESH)
        pl.semaphore_signal(barrier, inc=1, device_id={"src": zpos(j)}, device_id_type=MESH)
    pl.semaphore_signal(barrier, inc=1, device_id={"rel": 1 - r}, device_id_type=MESH)

    loads[0].wait()
    loads[1].wait()
    deg = jnp.broadcast_to(deg_in[...].astype(F32), (B, B)).T
    for slab in range(4):
        own[slab] = (grad[:, slab * B : (slab + 1) * B].astype(F32) / deg).astype(BF16)
    for n in (2, 3, 4):
        loads[n].wait()
    line = lax.broadcasted_iota(jnp.int32, (16, B), 0)
    place = jnp.full((16, B), -1, jnp.int32)
    for t in range(4):
        where_t = rows_in[0, t] * 4 + cols_in[0, t]
        place = jnp.where((line == t) & (t < count_in[0, 0]), where_t, place)
    meta[0, 4 * B : 4 * B + 16, :] = place.astype(F32).astype(BF16)
    scal[s, 0] = own[d]
    loads[5].wait()
    loads[6].wait()

    pl.semaphore_wait(barrier, 7)

    sent = []

    def go(copy):
        copy.start()
        sent.append(copy)
        return copy

    def chain(at, j, right):
        return to(
            scal.at[at, j], scal.at[at, j], (right_send if right else left_send).at[at, j],
            c_recv.at[at, j], src=zpos(1 if right else 3),
        )

    def push(j):
        @pl.when(s < 3)
        def _():
            chain(s, j, True).start()

        @pl.when(s > 0)
        def _():
            chain(s, j, False).start()

    def forward(n):
        for j in range(4):
            @pl.when(s >= n)
            def _():
                chain(zpos(4 - n), j, True).wait_recv()

            @pl.when((s >= n) & (s < 3))
            def _():
                chain(zpos(4 - n), j, True).start()

            @pl.when(s + n <= 3)
            def _():
                chain(zpos(n), j, False).wait_recv()

            @pl.when((s + n <= 3) & (s > 0))
            def _():
                chain(zpos(n), j, False).start()

    slab_y, slab_g, slab_k = [
        go(to(own.at[peer[j]], scal.at[s, j], a_send.at[j], a_recv.at[j], dst=peer[j]))
        for j in (2, 3, 1)
    ]
    push(0)
    tile_y = go(to(meta.at[0], meta.at[2], t_send.at[2], t_recv.at[2], dst=peer[2]))
    tile_k = go(to(meta.at[0], meta.at[1], t_send.at[1], t_recv.at[1], dst=peer[1]))
    feat_y = go(to(feats.at[0], feats.at[2], f_send.at[2], f_recv.at[2], dst=peer[2]))
    feat_k = go(to(feats.at[0], feats.at[1], f_send.at[1], f_recv.at[1], dst=peer[1]))
    slab_k.wait_recv()
    push(1)
    slab_y.wait_recv()
    push(2)
    slab_g.wait_recv()
    push(3)

    def densify(j):
        for k in range(4):
            for c in range(4):
                total = None
                for t in range(4):
                    code = meta[j, 4 * B + t : 4 * B + t + 1, :].astype(F32)
                    hit = jnp.where(code == (k * 4 + peer[c]).astype(F32), 1.0, 0.0).astype(BF16)
                    term = meta[j, t * B : (t + 1) * B, :] * hit
                    total = term if total is None else total + term
                dense[k, c * B : (c + 1) * B, j * B : (j + 1) * B] = total

    def add(at):
        total[...] += jnp.dot(dense[at], scal[at].reshape(4 * B, B), preferred_element_type=F32)

    def add_all(n):
        @pl.when(s >= n)
        def _():
            add(zpos(4 - n))

        @pl.when(s + n <= 3)
        def _():
            add(zpos(n))

    densify(0)
    tile_k.wait_recv()
    densify(1)
    forward(1)
    tile_y.wait_recv()
    tile_g = go(to(meta.at[2], meta.at[3], t_send.at[3], t_recv.at[3], dst=peer[1]))
    densify(2)
    forward(2)
    tile_g.wait_recv()
    densify(3)
    feat_y.wait_recv()
    feat_g = go(to(feats.at[2], feats.at[3], f_send.at[3], f_recv.at[3], dst=peer[1]))
    feat_k.wait_recv()
    for j in range(3):
        feats_t[:, :, j * B : (j + 1) * B] = feats[j].T.reshape(4, B, B)
    total[...] = jnp.zeros((4 * B, B), F32)
    add(s)
    add_all(1)
    add_all(2)
    feat_g.wait_recv()
    feats_t[:, :, 3 * B :] = feats[3].T.reshape(4, B, B)
    forward(3)
    add_all(3)
    for c in range(4):
        red[c] = total[c * B : (c + 1) * B, :]
    rows_f32[d] = red[0]
    rows = [
        go(to(red.at[j], rows_f32.at[d], r_send.at[j], r_recv.at[j], dst=peer[j]))
        for j in (1, 2, 3)
    ]
    high, low = split_high_low(total[...])
    parts = {}
    for j in (2, 1, 3, 0):
        left = feats_t[zpos(j)]
        wpart[j] = jnp.dot(left, high, preferred_element_type=F32) + jnp.dot(
            left, low, preferred_element_type=F32
        )
        if j:
            parts[j] = go(to(wpart.at[j], wrecv.at[j], d_send.at[j], d_recv.at[j], src=zpos(j)))
    for copy in rows:
        copy.wait_recv()
    loads[7].wait()
    value = None
    for c in range(4):
        right = weight[:, c * B : (c + 1) * B]
        for part in split_high_low(rows_f32[c]):
            term = lax.dot_general(part, right, (((1,), (1,)), ((), ())), preferred_element_type=F32)
            value = term if value is None else value + term
    mine[...] = value
    swap = go(to(mine, other, x_send.at[0], x_recv.at[0], rel=1 - r))
    block = wpart[0]
    for j in (1, 3, 2):
        parts[j].wait_recv()
    block = block + wrecv[1] + wrecv[2] + wrecv[3]
    final[d, s] = block.astype(BF16)

    along = [
        go(to(final.at[d, s], final.at[d, s], z_send.at[j], z_recv.at[j], src=zpos(j)))
        for j in (1, 2, 3)
    ]
    ys, ks, gs = [], [], []
    order = (0, 1, 3, 2)
    for j in order:
        if j:
            along[j - 1].wait_recv()
        at = final.at[d, zpos(4 - j)]
        ys.append(go(to(at, at, y_send.at[j], y_recv.at[j], dst=peer[2])))
        ks.append(go(to(at, at, k_send.at[j], k_recv.at[j], dst=peer[1])))
    for n, j in enumerate(order):
        ys[n].wait_recv()
        at = final.at[peer[2], zpos(4 - j)]
        gs.append(go(to(at, at, g_send.at[j], g_recv.at[j], dst=peer[1])))
    swap.wait_recv()
    fgrad_ref[...] = (mine[...] + other[...]).astype(BF16)
    for copy in ks + gs:
        copy.wait_recv()
    for slab in range(4):
        for q in range(4):
            wgrad_ref[q * B : (q + 1) * B, slab * B : (slab + 1) * B] = final[slab, q]
    for copy in sent:
        copy.wait_send()
    for n in range(3):
        for j in range(4):
            @pl.when((s >= n) & (s < 3))
            def _():
                chain(zpos(4 - n), j, True).wait_send()

            @pl.when((s + n <= 3) & (s > 0))
            def _():
                chain(zpos(n), j, False).wait_send()


def fast_body(features, out_grad, weights, tiles, tile_rows, tile_cols, tile_count, degrees):
    vmem = pl.BlockSpec(memory_space=pltpu.VMEM)
    sem = pltpu.SemaphoreType.DMA((4,))
    fgrad, wgrad = pl.pallas_call(
        kernel,
        out_shape=(
            jax.ShapeDtypeStruct((B, 4 * B), BF16),
            jax.ShapeDtypeStruct((4 * B, 4 * B), BF16),
        ),
        in_specs=[pl.BlockSpec(memory_space=pl.ANY)] * 8,
        out_specs=(vmem, vmem),
        scratch_shapes=[
            pltpu.VMEM((B, 4 * B), BF16),
            pltpu.VMEM((4 * B, 4 * B), BF16),
            pltpu.VMEM((1, B), jnp.int32),
            pltpu.SMEM((1, 4), jnp.int32),
            pltpu.SMEM((1, 4), jnp.int32),
            pltpu.SMEM((1, 1), jnp.int32),
            pltpu.VMEM((4 * B, B), F32),
            pltpu.VMEM((4, B, B), BF16),
            pltpu.VMEM((4, 4, B, B), BF16),
            pltpu.VMEM((4, 4 * B + 16, B), BF16),
            pltpu.VMEM((4, B, 4 * B), BF16),
            pltpu.VMEM((4, B, 4 * B), BF16),
            pltpu.VMEM((4, 4 * B, 4 * B), BF16),
            pltpu.VMEM((4, B, B), F32),
            pltpu.VMEM((4, B, B), F32),
            pltpu.VMEM((4, B, B), F32),
            pltpu.VMEM((4, B, B), F32),
            pltpu.VMEM((4, 4, B, B), BF16),
            pltpu.VMEM((B, 4 * B), F32),
            pltpu.VMEM((B, 4 * B), F32),
        ]
        + [pltpu.SemaphoreType.DMA((8,))]
        + [pltpu.SemaphoreType.DMA((4, 4))] * 3
        + [sem] * 20,
        compiler_params=pltpu.CompilerParams(
            collective_id=0, has_side_effects=True, vmem_limit_bytes=56 * 1024 * 1024
        ),
        cost_estimate=pl.CostEstimate(flops=10**9, bytes_accessed=4 * 10**6, transcendentals=0),
    )(features, out_grad, weights[0], tiles[0].reshape(4 * B, B), tile_rows, tile_cols, tile_count, degrees)
    return fgrad, wgrad.astype(F32)[None]


def body(features, out_grad, weights, tiles, tile_rows, tile_cols, tile_count, degrees):
    tile_size = tiles.shape[-1]
    width = features.shape[1]
    rows_dev = features.shape[0]
    n_dst = lax.axis_size("dst")
    n_cols = rows_dev * n_dst // tile_size
    group_size = 4
    scaled = (out_grad.astype(jnp.float32) / degrees[0].astype(jnp.float32)[:, None]).astype(
        jnp.bfloat16
    )
    panel = lax.all_gather(scaled, "src", axis=0, tiled=True)
    blocks = panel.reshape(-1, tile_size, width)
    live_count = tile_count[0, 0]

    def add_group(index, total):
        start = index * group_size
        tile_group = lax.dynamic_slice_in_dim(tiles[0], start, group_size, 0)
        row_group = lax.dynamic_slice_in_dim(tile_rows[0], start, group_size, 0)
        col_group = lax.dynamic_slice_in_dim(tile_cols[0], start, group_size, 0)
        picked = jnp.take(blocks, row_group, axis=0)
        contrib = jnp.einsum("gij,gjd->gid", tile_group, picked, preferred_element_type=jnp.float32)
        valid = (start + jnp.arange(group_size, dtype=jnp.int32) < live_count).astype(jnp.float32)
        return total.at[col_group].add(contrib * valid[:, None, None])

    n_groups = (live_count + group_size - 1) // group_size
    empty = jnp.zeros((n_cols, tile_size, width), jnp.float32)
    summed = lax.fori_loop(0, n_groups, add_group, empty)
    partial_value = summed.reshape(n_cols * tile_size, width)
    reduced = lax.psum_scatter(partial_value, "dst", scatter_dimension=0, tiled=True)
    local_weight = jnp.dot(features.astype(jnp.float32).T, reduced, precision=lax.Precision.HIGHEST)
    weight_grad = lax.psum(local_weight, ("src", "dst"))
    weight_wide = weights[0].astype(jnp.float32)
    own_part = jnp.dot(reduced, weight_wide.T, precision=lax.Precision.HIGHEST)
    feature_grad = lax.psum(own_part, "rel").astype(jnp.bfloat16)
    return (feature_grad, weight_grad[None])


def solution(mesh):
    in_specs = (
        P(("src", "dst"), None),
        P(("dst", "src"), None),
        P("rel", None, None),
        P("rel", ("src", "dst"), None, None),
        P("rel", ("src", "dst")),
        P("rel", ("src", "dst")),
        P("rel", ("src", "dst")),
        P("rel", ("dst", "src")),
    )
    out_specs = (P(("src", "dst"), None), P("rel", None, None))
    sizes = (mesh.shape["src"], mesh.shape["dst"], mesh.shape["rel"])

    def run(*args):
        features, tiles = args[0], args[3]
        shapes = (features.shape, tiles.shape)
        small = sizes == (4, 4, 2) and shapes == ((16 * B, 4 * B), (2, 64, B, B))
        chosen = fast_body if small else body
        return jax.shard_map(
            chosen, mesh=mesh, in_specs=in_specs, out_specs=out_specs, check_vma=False
        )(*args)

    return run
```

```python
import jax
import jax.numpy as jnp
from jax import lax
from jax.experimental import pallas as pl
from jax.experimental.pallas import tpu as pltpu
from jax.sharding import PartitionSpec as P

MESH = pl.DeviceIdType.MESH
B = 128
HALF = B // 2
F32, BF16 = jnp.float32, jnp.bfloat16


def split_high_low(x):
    high = x.astype(BF16)
    return high, (x - high.astype(F32)).astype(BF16)


def kernel(
    feat_ref, grad_ref, weight_ref, tiles_ref, rows_ref, cols_ref, count_ref, deg_ref,
    fgrad_ref, wgrad_ref,
    grad, weight, deg_in, rows_in, cols_in, count_in, total, own, scal, meta, feats, feats_t, dense, red, rows_f32, wpart, wrecv, final, mine, other,
    l_sem, right_send, left_send, c_recv, a_send, a_recv, t_send, t_recv, f_send, f_recv, d_send, d_recv,
    z_send, z_recv, y_send, y_recv, k_send, k_recv, g_send, g_recv, r_send, r_recv, x_send, x_recv,
):
    s, d, r = lax.axis_index("src"), lax.axis_index("dst"), lax.axis_index("rel")
    peer = (d, d + 1 - 2 * (d % 2), (d + 2) % 4, 3 - d)

    def zpos(step):
        return (s + step) % 4

    def to(source, target, send, recv, **device):
        return pltpu.make_async_remote_copy(
            src_ref=source, dst_ref=target, send_sem=send, recv_sem=recv,
            device_id=device, device_id_type=MESH,
        )

    loads = [
        pltpu.make_async_copy(source, target, l_sem.at[n])
        for n, (source, target) in enumerate((
            (grad_ref, grad), (deg_ref, deg_in), (rows_ref, rows_in), (cols_ref, cols_in),
            (count_ref, count_in), (tiles_ref, meta.at[0, pl.ds(0, 4 * B)]),
            (feat_ref, feats.at[0]), (weight_ref, weight),
        ))
    ]
    for copy in loads:
        copy.start()
    barrier = pltpu.get_barrier_semaphore()
    for j in (1, 2, 3):
        pl.semaphore_signal(barrier, inc=1, device_id={"dst": peer[j]}, device_id_type=MESH)
    pl.semaphore_signal(barrier, inc=1, device_id={"rel": 1 - r}, device_id_type=MESH)

    @pl.when(s < 3)
    def _():
        pl.semaphore_signal(barrier, inc=1, device_id={"src": zpos(1)}, device_id_type=MESH)

    @pl.when(s > 0)
    def _():
        pl.semaphore_signal(barrier, inc=1, device_id={"src": zpos(3)}, device_id_type=MESH)

    loads[0].wait()
    loads[1].wait()
    deg = jnp.broadcast_to(deg_in[...].astype(F32), (B, B)).T
    for slab in range(4):
        own[slab] = (grad[:, slab * B : (slab + 1) * B].astype(F32) / deg).astype(BF16)
    for n in (2, 3, 4):
        loads[n].wait()
    line = lax.broadcasted_iota(jnp.int32, (16, B), 0)
    place = jnp.full((16, B), -1, jnp.int32)
    for t in range(4):
        where_t = rows_in[0, t] * 4 + cols_in[0, t]
        place = jnp.where((line == t) & (t < count_in[0, 0]), where_t, place)
    meta[0, 4 * B : 4 * B + 16, :] = place.astype(F32).astype(BF16)
    scal[s, 0] = own[d]
    loads[5].wait()
    loads[6].wait()

    pl.semaphore_wait(barrier, 4 + (s + 3) // 4 + (6 - s) // 4)

    def densify(j):
        for k in range(4):
            for c in range(4):
                total = None
                for t in range(4):
                    code = meta[j, 4 * B + t : 4 * B + t + 1, :].astype(F32)
                    hit = jnp.where(code == (k * 4 + peer[c]).astype(F32), 1.0, 0.0).astype(BF16)
                    term = meta[j, t * B : (t + 1) * B, :] * hit
                    total = term if total is None else total + term
                dense[k, c * B : (c + 1) * B, j * B : (j + 1) * B] = total

    sent = []

    def go(copy):
        copy.start()
        sent.append(copy)
        return copy

    def chain(at, j, right):
        return to(
            scal.at[at, j], scal.at[at, j], (right_send if right else left_send).at[at, j],
            c_recv.at[at, j], src=zpos(1 if right else 3),
        )

    def push(j):
        @pl.when(s < 3)
        def _():
            chain(s, j, True).start()

        @pl.when(s > 0)
        def _():
            chain(s, j, False).start()

    def forward(n, *js):
        for j in js:
            @pl.when(s >= n)
            def _():
                chain(zpos(4 - n), j, True).wait_recv()

            @pl.when((s >= n) & (s < 3))
            def _():
                chain(zpos(4 - n), j, True).start()

            @pl.when(s + n <= 3)
            def _():
                chain(zpos(n), j, False).wait_recv()

            @pl.when((s + n <= 3) & (s > 0))
            def _():
                chain(zpos(n), j, False).start()

    slab_y, slab_g, slab_k = [
        go(to(own.at[peer[j]], scal.at[s, j], a_send.at[j], a_recv.at[j], dst=peer[j]))
        for j in (2, 3, 1)
    ]
    push(0)
    tile_y = go(to(meta.at[0], meta.at[2], t_send.at[2], t_recv.at[2], dst=peer[2]))
    tile_k = go(to(meta.at[0], meta.at[1], t_send.at[1], t_recv.at[1], dst=peer[1]))
    feat_y = go(to(feats.at[0], feats.at[2], f_send.at[2], f_recv.at[2], dst=peer[2]))
    feat_k = go(to(feats.at[0], feats.at[1], f_send.at[1], f_recv.at[1], dst=peer[1]))
    slab_k.wait_recv()
    push(1)
    densify(0)
    slab_y.wait_recv()
    push(2)
    slab_g.wait_recv()
    push(3)

    def add(at):
        total[...] += jnp.dot(dense[at], scal[at].reshape(4 * B, B), preferred_element_type=F32)

    def add_all(n):
        @pl.when(s >= n)
        def _():
            add(zpos(4 - n))

        @pl.when(s + n <= 3)
        def _():
            add(zpos(n))

    forward(1, 0, 1)
    tile_k.wait_recv()
    densify(1)
    forward(1, 2, 3)
    tile_y.wait_recv()
    tile_g = go(to(meta.at[2], meta.at[3], t_send.at[3], t_recv.at[3], dst=peer[1]))
    densify(2)
    forward(2, 0, 1, 2, 3)
    tile_g.wait_recv()
    densify(3)
    feat_y.wait_recv()
    feat_g = go(to(feats.at[2], feats.at[3], f_send.at[3], f_recv.at[3], dst=peer[1]))
    feat_k.wait_recv()
    for j in range(3):
        feats_t[:, :, j * B : (j + 1) * B] = feats[j].T.reshape(4, B, B)
    total[...] = jnp.zeros((4 * B, B), F32)
    add(s)
    add_all(1)
    add_all(2)
    feat_g.wait_recv()
    feats_t[:, :, 3 * B :] = feats[3].T.reshape(4, B, B)
    forward(3, 0, 1, 2, 3)
    add_all(3)
    for c in range(4):
        red[c] = total[c * B : (c + 1) * B, :]
    rows_f32[d] = red[0]
    rows = [
        go(to(red.at[j], rows_f32.at[d], r_send.at[j], r_recv.at[j], dst=peer[j]))
        for j in (1, 2, 3)
    ]
    high, low = split_high_low(total[...])
    parts = {}

    def part(j, h):
        at = pl.ds(h * HALF, HALF)
        return to(
            wpart.at[j, at], wrecv.at[j, at], d_send.at[j, h], d_recv.at[j, h], src=zpos(j)
        )

    for j in (2, 1, 3, 0):
        left = feats_t[zpos(j)]
        wpart[j] = jnp.dot(left, high, preferred_element_type=F32) + jnp.dot(
            left, low, preferred_element_type=F32
        )
        if j:
            parts[j, 0] = go(part(j, 0))
    for j in (2, 1, 3):
        parts[j, 1] = go(part(j, 1))
    for copy in rows:
        copy.wait_recv()
    loads[7].wait()
    value = None
    for c in range(4):
        right = weight[:, c * B : (c + 1) * B]
        for part in split_high_low(rows_f32[c]):
            term = lax.dot_general(part, right, (((1,), (1,)), ((), ())), preferred_element_type=F32)
            value = term if value is None else value + term
    mine[...] = value
    swap = go(to(mine, other, x_send.at[0], x_recv.at[0], rel=1 - r))
    order = (0, 1, 3, 2)
    along, ys, ks, gs = {}, {}, {}, {}

    def pass_on(j, h):
        at = final.at[d, zpos(4 - j), h]
        ys[j, h] = go(to(at, at, y_send.at[j, h], y_recv.at[j, h], dst=peer[2]))
        ks[j, h] = go(to(at, at, k_send.at[j, h], k_recv.at[j, h], dst=peer[1]))

    for h in range(2):
        rows_h = slice(h * HALF, (h + 1) * HALF)
        block = wpart[0, rows_h]
        for j in (1, 3, 2):
            parts[j, h].wait_recv()
        block = block + wrecv[1, rows_h] + wrecv[2, rows_h] + wrecv[3, rows_h]
        final[d, s, h] = block.astype(BF16)
        at = final.at[d, s, h]
        for j in (2, 1, 3):
            along[j, h] = go(to(at, at, z_send.at[j, h], z_recv.at[j, h], src=zpos(j)))
        pass_on(0, h)
    for h in range(2):
        for j in order:
            if j:
                along[j, h].wait_recv()
                pass_on(j, h)
            if h == 1:
                ys[j, 0].wait_recv()
                at = final.at[peer[2], zpos(4 - j), 0]
                gs[j, 0] = go(to(at, at, g_send.at[j, 0], g_recv.at[j, 0], dst=peer[1]))
    for j in order:
        ys[j, 1].wait_recv()
        at = final.at[peer[2], zpos(4 - j), 1]
        gs[j, 1] = go(to(at, at, g_send.at[j, 1], g_recv.at[j, 1], dst=peer[1]))
    swap.wait_recv()
    fgrad_ref[...] = (mine[...] + other[...]).astype(BF16)
    for copy in [*ks.values(), *gs.values()]:
        copy.wait_recv()
    for slab in range(4):
        for q in range(4):
            wgrad_ref[q * B : (q + 1) * B, slab * B : (slab + 1) * B] = final[slab, q].reshape(B, B)
    for copy in sent:
        copy.wait_send()
    for n in range(3):
        for j in range(4):
            @pl.when((s >= n) & (s < 3))
            def _():
                chain(zpos(4 - n), j, True).wait_send()

            @pl.when((s + n <= 3) & (s > 0))
            def _():
                chain(zpos(n), j, False).wait_send()


def fast_body(features, out_grad, weights, tiles, tile_rows, tile_cols, tile_count, degrees):
    vmem = pl.BlockSpec(memory_space=pltpu.VMEM)
    sem = pltpu.SemaphoreType.DMA((4,))
    fgrad, wgrad = pl.pallas_call(
        kernel,
        out_shape=(
            jax.ShapeDtypeStruct((B, 4 * B), BF16),
            jax.ShapeDtypeStruct((4 * B, 4 * B), BF16),
        ),
        in_specs=[pl.BlockSpec(memory_space=pl.ANY)] * 8,
        out_specs=(vmem, vmem),
        scratch_shapes=[
            pltpu.VMEM((B, 4 * B), BF16),
            pltpu.VMEM((4 * B, 4 * B), BF16),
            pltpu.VMEM((1, B), jnp.int32),
            pltpu.SMEM((1, 4), jnp.int32),
            pltpu.SMEM((1, 4), jnp.int32),
            pltpu.SMEM((1, 1), jnp.int32),
            pltpu.VMEM((4 * B, B), F32),
            pltpu.VMEM((4, B, B), BF16),
            pltpu.VMEM((4, 4, B, B), BF16),
            pltpu.VMEM((4, 4 * B + 16, B), BF16),
            pltpu.VMEM((4, B, 4 * B), BF16),
            pltpu.VMEM((4, B, 4 * B), BF16),
            pltpu.VMEM((4, 4 * B, 4 * B), BF16),
            pltpu.VMEM((4, B, B), F32),
            pltpu.VMEM((4, B, B), F32),
            pltpu.VMEM((4, B, B), F32),
            pltpu.VMEM((4, B, B), F32),
            pltpu.VMEM((4, 4, 2, HALF, B), BF16),
            pltpu.VMEM((B, 4 * B), F32),
            pltpu.VMEM((B, 4 * B), F32),
        ]
        + [pltpu.SemaphoreType.DMA((8,))]
        + [pltpu.SemaphoreType.DMA((4, 4))] * 3
        + [sem] * 6
        + [pltpu.SemaphoreType.DMA((4, 2))] * 10
        + [sem] * 4,
        compiler_params=pltpu.CompilerParams(
            collective_id=0, has_side_effects=True, vmem_limit_bytes=56 * 1024 * 1024
        ),
        cost_estimate=pl.CostEstimate(flops=10**9, bytes_accessed=4 * 10**6, transcendentals=0),
    )(features, out_grad, weights[0], tiles[0].reshape(4 * B, B), tile_rows, tile_cols, tile_count, degrees)
    return fgrad, wgrad.astype(F32)[None]


def body(features, out_grad, weights, tiles, tile_rows, tile_cols, tile_count, degrees):
    tile_size = tiles.shape[-1]
    width = features.shape[1]
    rows_dev = features.shape[0]
    n_dst = lax.axis_size("dst")
    n_cols = rows_dev * n_dst // tile_size
    group_size = 4
    scaled = (out_grad.astype(jnp.float32) / degrees[0].astype(jnp.float32)[:, None]).astype(
        jnp.bfloat16
    )
    panel = lax.all_gather(scaled, "src", axis=0, tiled=True)
    blocks = panel.reshape(-1, tile_size, width)
    live_count = tile_count[0, 0]

    def add_group(index, total):
        start = index * group_size
        tile_group = lax.dynamic_slice_in_dim(tiles[0], start, group_size, 0)
        row_group = lax.dynamic_slice_in_dim(tile_rows[0], start, group_size, 0)
        col_group = lax.dynamic_slice_in_dim(tile_cols[0], start, group_size, 0)
        picked = jnp.take(blocks, row_group, axis=0)
        contrib = jnp.einsum("gij,gjd->gid", tile_group, picked, preferred_element_type=jnp.float32)
        valid = (start + jnp.arange(group_size, dtype=jnp.int32) < live_count).astype(jnp.float32)
        return total.at[col_group].add(contrib * valid[:, None, None])

    n_groups = (live_count + group_size - 1) // group_size
    empty = jnp.zeros((n_cols, tile_size, width), jnp.float32)
    summed = lax.fori_loop(0, n_groups, add_group, empty)
    partial_value = summed.reshape(n_cols * tile_size, width)
    reduced = lax.psum_scatter(partial_value, "dst", scatter_dimension=0, tiled=True)
    local_weight = jnp.dot(features.astype(jnp.float32).T, reduced, precision=lax.Precision.HIGHEST)
    weight_grad = lax.psum(local_weight, ("src", "dst"))
    weight_wide = weights[0].astype(jnp.float32)
    own_part = jnp.dot(reduced, weight_wide.T, precision=lax.Precision.HIGHEST)
    feature_grad = lax.psum(own_part, "rel").astype(jnp.bfloat16)
    return (feature_grad, weight_grad[None])


def solution(mesh):
    in_specs = (
        P(("src", "dst"), None),
        P(("dst", "src"), None),
        P("rel", None, None),
        P("rel", ("src", "dst"), None, None),
        P("rel", ("src", "dst")),
        P("rel", ("src", "dst")),
        P("rel", ("src", "dst")),
        P("rel", ("dst", "src")),
    )
    out_specs = (P(("src", "dst"), None), P("rel", None, None))
    sizes = (mesh.shape["src"], mesh.shape["dst"], mesh.shape["rel"])

    def run(*args):
        features, tiles = args[0], args[3]
        shapes = (features.shape, tiles.shape)
        small = sizes == (4, 4, 2) and shapes == ((16 * B, 4 * B), (2, 64, B, B))
        chosen = fast_body if small else body
        return jax.shard_map(
            chosen, mesh=mesh, in_specs=in_specs, out_specs=out_specs, check_vma=False
        )(*args)

    return run
```

```python
import jax
import jax.numpy as jnp
from jax import lax
from jax.experimental import pallas as pl
from jax.experimental.pallas import tpu as pltpu
from jax.sharding import PartitionSpec as P

MESH = pl.DeviceIdType.MESH
B = 128
F32, BF16 = jnp.float32, jnp.bfloat16


def split_high_low(x):
    high = x.astype(BF16)
    return high, (x - high.astype(F32)).astype(BF16)


def kernel(
    feat_ref, grad_ref, weight_ref, tiles_ref, rows_ref, cols_ref, count_ref, deg_ref,
    fgrad_ref, wgrad_ref,
    grad, weight, deg_in, rows_in, cols_in, count_in, total, own, scal, meta, feats, feats_t, dense, red, rows_f32, wpart, wrecv, final, mine, other,
    l_sem, right_send, left_send, c_recv, a_send, a_recv, t_send, t_recv, f_send, f_recv, d_send, d_recv,
    z_send, z_recv, y_send, y_recv, k_send, k_recv, g_send, g_recv, r_send, r_recv, x_send, x_recv,
):
    s, d, r = lax.axis_index("src"), lax.axis_index("dst"), lax.axis_index("rel")
    peer = (d, d + 1 - 2 * (d % 2), (d + 2) % 4, 3 - d)

    def zpos(step):
        return (s + step) % 4

    def to(source, target, send, recv, **device):
        return pltpu.make_async_remote_copy(
            src_ref=source, dst_ref=target, send_sem=send, recv_sem=recv,
            device_id=device, device_id_type=MESH,
        )

    loads = [
        pltpu.make_async_copy(source, target, l_sem.at[n])
        for n, (source, target) in enumerate((
            (grad_ref, grad), (deg_ref, deg_in), (rows_ref, rows_in), (cols_ref, cols_in),
            (count_ref, count_in), (tiles_ref, meta.at[0, pl.ds(0, 4 * B)]),
            (feat_ref, feats.at[0]), (weight_ref, weight),
        ))
    ]
    for copy in loads:
        copy.start()
    barrier = pltpu.get_barrier_semaphore()
    for j in (1, 2, 3):
        pl.semaphore_signal(barrier, inc=1, device_id={"dst": peer[j]}, device_id_type=MESH)
    pl.semaphore_signal(barrier, inc=1, device_id={"rel": 1 - r}, device_id_type=MESH)

    @pl.when(s < 3)
    def _():
        pl.semaphore_signal(barrier, inc=1, device_id={"src": zpos(1)}, device_id_type=MESH)

    @pl.when(s > 0)
    def _():
        pl.semaphore_signal(barrier, inc=1, device_id={"src": zpos(3)}, device_id_type=MESH)

    loads[0].wait()
    loads[1].wait()
    deg = jnp.broadcast_to(deg_in[...].astype(F32), (B, B)).T
    for slab in range(4):
        own[slab] = (grad[:, slab * B : (slab + 1) * B].astype(F32) / deg).astype(BF16)
    for n in (2, 3, 4):
        loads[n].wait()
    line = lax.broadcasted_iota(jnp.int32, (16, B), 0)
    place = jnp.full((16, B), -1, jnp.int32)
    for t in range(4):
        where_t = rows_in[0, t] * 4 + cols_in[0, t]
        place = jnp.where((line == t) & (t < count_in[0, 0]), where_t, place)
    meta[0, 4 * B : 4 * B + 16, :] = place.astype(F32).astype(BF16)
    scal[s, 0] = own[d]
    loads[5].wait()
    loads[6].wait()

    pl.semaphore_wait(barrier, 4 + (s + 3) // 4 + (6 - s) // 4)

    def densify(j):
        for k in range(4):
            for c in range(4):
                total = None
                for t in range(4):
                    code = meta[j, 4 * B + t : 4 * B + t + 1, :].astype(F32)
                    hit = jnp.where(code == (k * 4 + peer[c]).astype(F32), 1.0, 0.0).astype(BF16)
                    term = meta[j, t * B : (t + 1) * B, :] * hit
                    total = term if total is None else total + term
                dense[k, c * B : (c + 1) * B, j * B : (j + 1) * B] = total

    sent = []

    def go(copy):
        copy.start()
        sent.append(copy)
        return copy

    def chain(at, j, right):
        return to(
            scal.at[at, j], scal.at[at, j], (right_send if right else left_send).at[at, j],
            c_recv.at[at, j], src=zpos(1 if right else 3),
        )

    def push(j):
        @pl.when(s < 3)
        def _():
            chain(s, j, True).start()

        @pl.when(s > 0)
        def _():
            chain(s, j, False).start()

    def forward(n, *js):
        for j in js:
            @pl.when(s >= n)
            def _():
                chain(zpos(4 - n), j, True).wait_recv()

            @pl.when((s >= n) & (s < 3))
            def _():
                chain(zpos(4 - n), j, True).start()

            @pl.when(s + n <= 3)
            def _():
                chain(zpos(n), j, False).wait_recv()

            @pl.when((s + n <= 3) & (s > 0))
            def _():
                chain(zpos(n), j, False).start()

    slab_y, slab_g, slab_k = [
        go(to(own.at[peer[j]], scal.at[s, j], a_send.at[j], a_recv.at[j], dst=peer[j]))
        for j in (2, 3, 1)
    ]
    push(0)
    tile_y = go(to(meta.at[0], meta.at[2], t_send.at[2], t_recv.at[2], dst=peer[2]))
    tile_k = go(to(meta.at[0], meta.at[1], t_send.at[1], t_recv.at[1], dst=peer[1]))
    feat_y = go(to(feats.at[0], feats.at[2], f_send.at[2], f_recv.at[2], dst=peer[2]))
    feat_k = go(to(feats.at[0], feats.at[1], f_send.at[1], f_recv.at[1], dst=peer[1]))
    slab_k.wait_recv()
    push(1)
    densify(0)
    slab_y.wait_recv()
    push(2)
    slab_g.wait_recv()
    push(3)

    def add(at):
        total[...] += jnp.dot(dense[at], scal[at].reshape(4 * B, B), preferred_element_type=F32)

    def add_all(n):
        @pl.when(s >= n)
        def _():
            add(zpos(4 - n))

        @pl.when(s + n <= 3)
        def _():
            add(zpos(n))

    forward(1, 0, 1)
    tile_k.wait_recv()
    densify(1)
    forward(1, 2, 3)
    tile_y.wait_recv()
    tile_g = go(to(meta.at[2], meta.at[3], t_send.at[3], t_recv.at[3], dst=peer[1]))
    densify(2)
    forward(2, 0, 1, 2, 3)
    tile_g.wait_recv()
    densify(3)
    feat_y.wait_recv()
    feat_g = go(to(feats.at[2], feats.at[3], f_send.at[3], f_recv.at[3], dst=peer[1]))
    feat_k.wait_recv()
    for j in range(3):
        feats_t[:, :, j * B : (j + 1) * B] = feats[j].T.reshape(4, B, B)
    total[...] = jnp.zeros((4 * B, B), F32)
    add(s)
    add_all(1)
    add_all(2)
    feat_g.wait_recv()
    feats_t[:, :, 3 * B :] = feats[3].T.reshape(4, B, B)
    forward(3, 0, 1, 2, 3)
    add_all(3)
    for c in range(4):
        red[c] = total[c * B : (c + 1) * B, :]
    high, low = split_high_low(total[...])
    parts = {}
    for j in (2, 1, 3, 0):
        left = feats_t[zpos(j)]
        wpart[j] = jnp.dot(left, high, preferred_element_type=F32) + jnp.dot(
            left, low, preferred_element_type=F32
        )
        if j:
            parts[j] = go(to(wpart.at[j], wrecv.at[j], d_send.at[j], d_recv.at[j], src=zpos(j)))
    rows_f32[d] = red[0]
    rows = [
        go(to(red.at[j], rows_f32.at[d], r_send.at[j], r_recv.at[j], dst=peer[j]))
        for j in (1, 2, 3)
    ]
    for copy in rows:
        copy.wait_recv()
    loads[7].wait()
    value = None
    for c in range(4):
        right = weight[:, c * B : (c + 1) * B]
        for part in split_high_low(rows_f32[c]):
            term = lax.dot_general(part, right, (((1,), (1,)), ((), ())), preferred_element_type=F32)
            value = term if value is None else value + term
    mine[...] = value
    swap = go(to(mine, other, x_send.at[0], x_recv.at[0], rel=1 - r))
    block = wpart[0]
    for j in (1, 3, 2):
        parts[j].wait_recv()
    block = block + wrecv[1] + wrecv[2] + wrecv[3]
    final[d, s] = block.astype(BF16)

    along = [
        go(to(final.at[d, s], final.at[d, s], z_send.at[j], z_recv.at[j], src=zpos(j)))
        for j in (1, 2, 3)
    ]
    ys, ks, gs = [], [], []
    order = (0, 1, 3, 2)
    for j in order:
        if j:
            along[j - 1].wait_recv()
        at = final.at[d, zpos(4 - j)]
        ys.append(go(to(at, at, y_send.at[j], y_recv.at[j], dst=peer[2])))
        ks.append(go(to(at, at, k_send.at[j], k_recv.at[j], dst=peer[1])))
    for n, j in enumerate(order):
        ys[n].wait_recv()
        at = final.at[peer[2], zpos(4 - j)]
        gs.append(go(to(at, at, g_send.at[j], g_recv.at[j], dst=peer[1])))
    swap.wait_recv()
    fgrad_ref[...] = (mine[...] + other[...]).astype(BF16)
    for copy in ks + gs:
        copy.wait_recv()
    for slab in range(4):
        for q in range(4):
            wgrad_ref[q * B : (q + 1) * B, slab * B : (slab + 1) * B] = final[slab, q]
    for copy in sent:
        copy.wait_send()
    for n in range(3):
        for j in range(4):
            @pl.when((s >= n) & (s < 3))
            def _():
                chain(zpos(4 - n), j, True).wait_send()

            @pl.when((s + n <= 3) & (s > 0))
            def _():
                chain(zpos(n), j, False).wait_send()


def fast_body(features, out_grad, weights, tiles, tile_rows, tile_cols, tile_count, degrees):
    vmem = pl.BlockSpec(memory_space=pltpu.VMEM)
    sem = pltpu.SemaphoreType.DMA((4,))
    fgrad, wgrad = pl.pallas_call(
        kernel,
        out_shape=(
            jax.ShapeDtypeStruct((B, 4 * B), BF16),
            jax.ShapeDtypeStruct((4 * B, 4 * B), BF16),
        ),
        in_specs=[pl.BlockSpec(memory_space=pl.ANY)] * 8,
        out_specs=(vmem, vmem),
        scratch_shapes=[
            pltpu.VMEM((B, 4 * B), BF16),
            pltpu.VMEM((4 * B, 4 * B), BF16),
            pltpu.VMEM((1, B), jnp.int32),
            pltpu.SMEM((1, 4), jnp.int32),
            pltpu.SMEM((1, 4), jnp.int32),
            pltpu.SMEM((1, 1), jnp.int32),
            pltpu.VMEM((4 * B, B), F32),
            pltpu.VMEM((4, B, B), BF16),
            pltpu.VMEM((4, 4, B, B), BF16),
            pltpu.VMEM((4, 4 * B + 16, B), BF16),
            pltpu.VMEM((4, B, 4 * B), BF16),
            pltpu.VMEM((4, B, 4 * B), BF16),
            pltpu.VMEM((4, 4 * B, 4 * B), BF16),
            pltpu.VMEM((4, B, B), F32),
            pltpu.VMEM((4, B, B), F32),
            pltpu.VMEM((4, B, B), F32),
            pltpu.VMEM((4, B, B), F32),
            pltpu.VMEM((4, 4, B, B), BF16),
            pltpu.VMEM((B, 4 * B), F32),
            pltpu.VMEM((B, 4 * B), F32),
        ]
        + [pltpu.SemaphoreType.DMA((8,))]
        + [pltpu.SemaphoreType.DMA((4, 4))] * 3
        + [sem] * 20,
        compiler_params=pltpu.CompilerParams(
            collective_id=0, has_side_effects=True, vmem_limit_bytes=56 * 1024 * 1024
        ),
        cost_estimate=pl.CostEstimate(flops=10**9, bytes_accessed=4 * 10**6, transcendentals=0),
    )(features, out_grad, weights[0], tiles[0].reshape(4 * B, B), tile_rows, tile_cols, tile_count, degrees)
    return fgrad, wgrad.astype(F32)[None]


def body(features, out_grad, weights, tiles, tile_rows, tile_cols, tile_count, degrees):
    tile_size = tiles.shape[-1]
    width = features.shape[1]
    rows_dev = features.shape[0]
    n_dst = lax.axis_size("dst")
    n_cols = rows_dev * n_dst // tile_size
    group_size = 4
    scaled = (out_grad.astype(jnp.float32) / degrees[0].astype(jnp.float32)[:, None]).astype(
        jnp.bfloat16
    )
    panel = lax.all_gather(scaled, "src", axis=0, tiled=True)
    blocks = panel.reshape(-1, tile_size, width)
    live_count = tile_count[0, 0]

    def add_group(index, total):
        start = index * group_size
        tile_group = lax.dynamic_slice_in_dim(tiles[0], start, group_size, 0)
        row_group = lax.dynamic_slice_in_dim(tile_rows[0], start, group_size, 0)
        col_group = lax.dynamic_slice_in_dim(tile_cols[0], start, group_size, 0)
        picked = jnp.take(blocks, row_group, axis=0)
        contrib = jnp.einsum("gij,gjd->gid", tile_group, picked, preferred_element_type=jnp.float32)
        valid = (start + jnp.arange(group_size, dtype=jnp.int32) < live_count).astype(jnp.float32)
        return total.at[col_group].add(contrib * valid[:, None, None])

    n_groups = (live_count + group_size - 1) // group_size
    empty = jnp.zeros((n_cols, tile_size, width), jnp.float32)
    summed = lax.fori_loop(0, n_groups, add_group, empty)
    partial_value = summed.reshape(n_cols * tile_size, width)
    reduced = lax.psum_scatter(partial_value, "dst", scatter_dimension=0, tiled=True)
    local_weight = jnp.dot(features.astype(jnp.float32).T, reduced, precision=lax.Precision.HIGHEST)
    weight_grad = lax.psum(local_weight, ("src", "dst"))
    weight_wide = weights[0].astype(jnp.float32)
    own_part = jnp.dot(reduced, weight_wide.T, precision=lax.Precision.HIGHEST)
    feature_grad = lax.psum(own_part, "rel").astype(jnp.bfloat16)
    return (feature_grad, weight_grad[None])


def solution(mesh):
    in_specs = (
        P(("src", "dst"), None),
        P(("dst", "src"), None),
        P("rel", None, None),
        P("rel", ("src", "dst"), None, None),
        P("rel", ("src", "dst")),
        P("rel", ("src", "dst")),
        P("rel", ("src", "dst")),
        P("rel", ("dst", "src")),
    )
    out_specs = (P(("src", "dst"), None), P("rel", None, None))
    sizes = (mesh.shape["src"], mesh.shape["dst"], mesh.shape["rel"])

    def run(*args):
        features, tiles = args[0], args[3]
        shapes = (features.shape, tiles.shape)
        small = sizes == (4, 4, 2) and shapes == ((16 * B, 4 * B), (2, 64, B, B))
        chosen = fast_body if small else body
        return jax.shard_map(
            chosen, mesh=mesh, in_specs=in_specs, out_specs=out_specs, check_vma=False
        )(*args)

    return run
```

```python
import jax
import jax.numpy as jnp
from jax import lax
from jax.experimental import pallas as pl
from jax.experimental.pallas import tpu as pltpu
from jax.sharding import PartitionSpec as P

MESH = pl.DeviceIdType.MESH
B = 128
F32, BF16 = jnp.float32, jnp.bfloat16


def split_high_low(x):
    high = x.astype(BF16)
    return high, (x - high.astype(F32)).astype(BF16)


def kernel(
    feat_ref, grad_ref, weight_ref, tiles_ref, rows_ref, cols_ref, count_ref, deg_ref,
    fgrad_ref, wgrad_ref,
    grad, weight, deg_in, rows_in, cols_in, count_in, total, own, scal, meta, feats, feats_t, dense, red, rows_f32, wpart, wrecv, final, mine, other,
    l_sem, right_send, left_send, c_recv, a_send, a_recv, t_send, t_recv, f_send, f_recv, d_send, d_recv,
    z_send, z_recv, y_send, y_recv, k_send, k_recv, g_send, g_recv, r_send, r_recv, x_send, x_recv,
):
    s, d, r = lax.axis_index("src"), lax.axis_index("dst"), lax.axis_index("rel")
    peer = (d, d + 1 - 2 * (d % 2), (d + 2) % 4, 3 - d)

    def zpos(step):
        return (s + step) % 4

    def to(source, target, send, recv, **device):
        return pltpu.make_async_remote_copy(
            src_ref=source, dst_ref=target, send_sem=send, recv_sem=recv,
            device_id=device, device_id_type=MESH,
        )

    loads = [
        pltpu.make_async_copy(source, target, l_sem.at[n])
        for n, (source, target) in enumerate((
            (grad_ref, grad), (deg_ref, deg_in), (rows_ref, rows_in), (cols_ref, cols_in),
            (count_ref, count_in), (tiles_ref, meta.at[0, pl.ds(0, 4 * B)]),
            (feat_ref, feats.at[0]), (weight_ref, weight),
        ))
    ]
    for copy in loads:
        copy.start()
    barrier = pltpu.get_barrier_semaphore()
    for j in (1, 2, 3):
        pl.semaphore_signal(barrier, inc=1, device_id={"dst": peer[j]}, device_id_type=MESH)
    pl.semaphore_signal(barrier, inc=1, device_id={"rel": 1 - r}, device_id_type=MESH)

    @pl.when(s < 3)
    def _():
        pl.semaphore_signal(barrier, inc=1, device_id={"src": zpos(1)}, device_id_type=MESH)

    @pl.when(s > 0)
    def _():
        pl.semaphore_signal(barrier, inc=1, device_id={"src": zpos(3)}, device_id_type=MESH)

    loads[0].wait()
    loads[1].wait()
    deg = jnp.broadcast_to(deg_in[...].astype(F32), (B, B)).T
    for slab in range(4):
        own[slab] = (grad[:, slab * B : (slab + 1) * B].astype(F32) / deg).astype(BF16)
    for n in (2, 3, 4):
        loads[n].wait()
    line = lax.broadcasted_iota(jnp.int32, (16, B), 0)
    place = jnp.full((16, B), -1, jnp.int32)
    for t in range(4):
        where_t = rows_in[0, t] * 4 + cols_in[0, t]
        place = jnp.where((line == t) & (t < count_in[0, 0]), where_t, place)
    meta[0, 4 * B : 4 * B + 16, :] = place.astype(F32).astype(BF16)
    scal[s, 0] = own[d]
    loads[5].wait()
    loads[6].wait()

    pl.semaphore_wait(barrier, 4 + (s + 3) // 4 + (6 - s) // 4)

    def densify(j):
        for k in range(4):
            for c in range(4):
                total = None
                for t in range(4):
                    code = meta[j, 4 * B + t : 4 * B + t + 1, :].astype(F32)
                    hit = jnp.where(code == (k * 4 + peer[c]).astype(F32), 1.0, 0.0).astype(BF16)
                    term = meta[j, t * B : (t + 1) * B, :] * hit
                    total = term if total is None else total + term
                dense[k, c * B : (c + 1) * B, j * B : (j + 1) * B] = total

    sent = []

    def go(copy):
        copy.start()
        sent.append(copy)
        return copy

    def chain(at, j, right):
        return to(
            scal.at[at, j], scal.at[at, j], (right_send if right else left_send).at[at, j],
            c_recv.at[at, j], src=zpos(1 if right else 3),
        )

    def push(j):
        @pl.when(s < 3)
        def _():
            chain(s, j, True).start()

        @pl.when(s > 0)
        def _():
            chain(s, j, False).start()

    def forward(n, *js):
        for j in js:
            @pl.when(s >= n)
            def _():
                chain(zpos(4 - n), j, True).wait_recv()

            @pl.when((s >= n) & (s < 3))
            def _():
                chain(zpos(4 - n), j, True).start()

            @pl.when(s + n <= 3)
            def _():
                chain(zpos(n), j, False).wait_recv()

            @pl.when((s + n <= 3) & (s > 0))
            def _():
                chain(zpos(n), j, False).start()

    slab_y, slab_g, slab_k = [
        go(to(own.at[peer[j]], scal.at[s, j], a_send.at[j], a_recv.at[j], dst=peer[j]))
        for j in (2, 3, 1)
    ]
    push(0)
    tile_y = go(to(meta.at[0], meta.at[2], t_send.at[2], t_recv.at[2], dst=peer[2]))
    tile_k = go(to(meta.at[0], meta.at[1], t_send.at[1], t_recv.at[1], dst=peer[1]))
    feat_y = go(to(feats.at[0], feats.at[2], f_send.at[2], f_recv.at[2], dst=peer[2]))
    feat_k = go(to(feats.at[0], feats.at[1], f_send.at[1], f_recv.at[1], dst=peer[1]))
    slab_k.wait_recv()
    push(1)
    densify(0)
    slab_y.wait_recv()
    push(2)
    slab_g.wait_recv()
    push(3)

    def add(at):
        total[...] += jnp.dot(dense[at], scal[at].reshape(4 * B, B), preferred_element_type=F32)

    def add_all(n):
        @pl.when(s >= n)
        def _():
            add(zpos(4 - n))

        @pl.when(s + n <= 3)
        def _():
            add(zpos(n))

    forward(1, 0, 1)
    tile_k.wait_recv()
    densify(1)
    forward(1, 2, 3)
    tile_y.wait_recv()
    tile_g = go(to(meta.at[2], meta.at[3], t_send.at[3], t_recv.at[3], dst=peer[1]))
    densify(2)
    forward(2, 0, 1, 2, 3)
    tile_g.wait_recv()
    densify(3)
    feat_y.wait_recv()
    feat_g = go(to(feats.at[2], feats.at[3], f_send.at[3], f_recv.at[3], dst=peer[1]))
    feat_k.wait_recv()
    for j in range(3):
        feats_t[:, :, j * B : (j + 1) * B] = feats[j].T.reshape(4, B, B)
    total[...] = jnp.zeros((4 * B, B), F32)
    add(s)
    add_all(1)
    add_all(2)
    feat_g.wait_recv()
    feats_t[:, :, 3 * B :] = feats[3].T.reshape(4, B, B)
    forward(3, 0, 1, 2, 3)
    add_all(3)
    for c in range(4):
        red[c] = total[c * B : (c + 1) * B, :]
    high, low = split_high_low(total[...])
    parts = {}
    for j in (2, 1, 3, 0):
        left = feats_t[zpos(j)]
        wpart[j] = jnp.dot(left, high, preferred_element_type=F32) + jnp.dot(
            left, low, preferred_element_type=F32
        )
        if j:
            parts[j] = go(to(wpart.at[j], wrecv.at[j], d_send.at[j], d_recv.at[j], src=zpos(j)))
    rows_f32[d] = red[0]
    rows = [
        go(to(red.at[j], rows_f32.at[d], r_send.at[j], r_recv.at[j], dst=peer[j]))
        for j in (1, 2, 3)
    ]
    for copy in rows:
        copy.wait_recv()
    loads[7].wait()
    value = None
    for c in range(4):
        right = weight[:, c * B : (c + 1) * B]
        for part in split_high_low(rows_f32[c]):
            term = lax.dot_general(part, right, (((1,), (1,)), ((), ())), preferred_element_type=F32)
            value = term if value is None else value + term
    mine[...] = value
    swap = go(to(mine, other, x_send.at[0], x_recv.at[0], rel=1 - r))
    block = wpart[0]
    for j in (1, 3, 2):
        parts[j].wait_recv()
    block = block + wrecv[1] + wrecv[2] + wrecv[3]
    final[d, s] = block.astype(BF16)

    along = [
        go(to(final.at[d, s], final.at[d, s], z_send.at[j], z_recv.at[j], src=zpos(j)))
        for j in (1, 2, 3)
    ]
    ys, ks, gs = [], [], []
    order = (0, 1, 3, 2)
    for j in order:
        if j:
            along[j - 1].wait_recv()
        at = final.at[d, zpos(4 - j)]
        ys.append(go(to(at, at, y_send.at[j], y_recv.at[j], dst=peer[2])))
        ks.append(go(to(at, at, k_send.at[j], k_recv.at[j], dst=peer[1])))
    for n, j in enumerate(order):
        ys[n].wait_recv()
        at = final.at[peer[2], zpos(4 - j)]
        gs.append(go(to(at, at, g_send.at[j], g_recv.at[j], dst=peer[1])))
    swap.wait_recv()
    fgrad_ref[...] = (mine[...] + other[...]).astype(BF16)
    def lay_out(slab):
        at = pl.ds(pl.multiple_of(slab * B, B), B)
        for q in range(4):
            wgrad_ref[q * B : (q + 1) * B, at] = final[slab, q]

    lay_out(d)
    lay_out(peer[2])
    for copy in ks:
        copy.wait_recv()
    lay_out(peer[1])
    for copy in gs:
        copy.wait_recv()
    lay_out(peer[3])
    for copy in sent:
        copy.wait_send()
    for n in range(3):
        for j in range(4):
            @pl.when((s >= n) & (s < 3))
            def _():
                chain(zpos(4 - n), j, True).wait_send()

            @pl.when((s + n <= 3) & (s > 0))
            def _():
                chain(zpos(n), j, False).wait_send()


def fast_body(features, out_grad, weights, tiles, tile_rows, tile_cols, tile_count, degrees):
    vmem = pl.BlockSpec(memory_space=pltpu.VMEM)
    sem = pltpu.SemaphoreType.DMA((4,))
    fgrad, wgrad = pl.pallas_call(
        kernel,
        out_shape=(
            jax.ShapeDtypeStruct((B, 4 * B), BF16),
            jax.ShapeDtypeStruct((4 * B, 4 * B), BF16),
        ),
        in_specs=[pl.BlockSpec(memory_space=pl.ANY)] * 8,
        out_specs=(vmem, vmem),
        scratch_shapes=[
            pltpu.VMEM((B, 4 * B), BF16),
            pltpu.VMEM((4 * B, 4 * B), BF16),
            pltpu.VMEM((1, B), jnp.int32),
            pltpu.SMEM((1, 4), jnp.int32),
            pltpu.SMEM((1, 4), jnp.int32),
            pltpu.SMEM((1, 1), jnp.int32),
            pltpu.VMEM((4 * B, B), F32),
            pltpu.VMEM((4, B, B), BF16),
            pltpu.VMEM((4, 4, B, B), BF16),
            pltpu.VMEM((4, 4 * B + 16, B), BF16),
            pltpu.VMEM((4, B, 4 * B), BF16),
            pltpu.VMEM((4, B, 4 * B), BF16),
            pltpu.VMEM((4, 4 * B, 4 * B), BF16),
            pltpu.VMEM((4, B, B), F32),
            pltpu.VMEM((4, B, B), F32),
            pltpu.VMEM((4, B, B), F32),
            pltpu.VMEM((4, B, B), F32),
            pltpu.VMEM((4, 4, B, B), BF16),
            pltpu.VMEM((B, 4 * B), F32),
            pltpu.VMEM((B, 4 * B), F32),
        ]
        + [pltpu.SemaphoreType.DMA((8,))]
        + [pltpu.SemaphoreType.DMA((4, 4))] * 3
        + [sem] * 20,
        compiler_params=pltpu.CompilerParams(
            collective_id=0, has_side_effects=True, vmem_limit_bytes=56 * 1024 * 1024
        ),
        cost_estimate=pl.CostEstimate(flops=10**9, bytes_accessed=4 * 10**6, transcendentals=0),
    )(features, out_grad, weights[0], tiles[0].reshape(4 * B, B), tile_rows, tile_cols, tile_count, degrees)
    return fgrad, wgrad.astype(F32)[None]


def body(features, out_grad, weights, tiles, tile_rows, tile_cols, tile_count, degrees):
    tile_size = tiles.shape[-1]
    width = features.shape[1]
    rows_dev = features.shape[0]
    n_dst = lax.axis_size("dst")
    n_cols = rows_dev * n_dst // tile_size
    group_size = 4
    scaled = (out_grad.astype(jnp.float32) / degrees[0].astype(jnp.float32)[:, None]).astype(
        jnp.bfloat16
    )
    panel = lax.all_gather(scaled, "src", axis=0, tiled=True)
    blocks = panel.reshape(-1, tile_size, width)
    live_count = tile_count[0, 0]

    def add_group(index, total):
        start = index * group_size
        tile_group = lax.dynamic_slice_in_dim(tiles[0], start, group_size, 0)
        row_group = lax.dynamic_slice_in_dim(tile_rows[0], start, group_size, 0)
        col_group = lax.dynamic_slice_in_dim(tile_cols[0], start, group_size, 0)
        picked = jnp.take(blocks, row_group, axis=0)
        contrib = jnp.einsum("gij,gjd->gid", tile_group, picked, preferred_element_type=jnp.float32)
        valid = (start + jnp.arange(group_size, dtype=jnp.int32) < live_count).astype(jnp.float32)
        return total.at[col_group].add(contrib * valid[:, None, None])

    n_groups = (live_count + group_size - 1) // group_size
    empty = jnp.zeros((n_cols, tile_size, width), jnp.float32)
    summed = lax.fori_loop(0, n_groups, add_group, empty)
    partial_value = summed.reshape(n_cols * tile_size, width)
    reduced = lax.psum_scatter(partial_value, "dst", scatter_dimension=0, tiled=True)
    local_weight = jnp.dot(features.astype(jnp.float32).T, reduced, precision=lax.Precision.HIGHEST)
    weight_grad = lax.psum(local_weight, ("src", "dst"))
    weight_wide = weights[0].astype(jnp.float32)
    own_part = jnp.dot(reduced, weight_wide.T, precision=lax.Precision.HIGHEST)
    feature_grad = lax.psum(own_part, "rel").astype(jnp.bfloat16)
    return (feature_grad, weight_grad[None])


def solution(mesh):
    in_specs = (
        P(("src", "dst"), None),
        P(("dst", "src"), None),
        P("rel", None, None),
        P("rel", ("src", "dst"), None, None),
        P("rel", ("src", "dst")),
        P("rel", ("src", "dst")),
        P("rel", ("src", "dst")),
        P("rel", ("dst", "src")),
    )
    out_specs = (P(("src", "dst"), None), P("rel", None, None))
    sizes = (mesh.shape["src"], mesh.shape["dst"], mesh.shape["rel"])

    def run(*args):
        features, tiles = args[0], args[3]
        shapes = (features.shape, tiles.shape)
        small = sizes == (4, 4, 2) and shapes == ((16 * B, 4 * B), (2, 64, B, B))
        chosen = fast_body if small else body
        return jax.shard_map(
            chosen, mesh=mesh, in_specs=in_specs, out_specs=out_specs, check_vma=False
        )(*args)

    return run
```
